1024 devices in a mesh: dp: 128 (over z_lo, x, core), group: 8 (over z_hi, y).
Axes of the slice: x: 4, y: 4, z: 32 (z_hi: 2, z_lo: 16; z = z_hi * 16 + z_lo), core: 2. Of those that a mesh axis runs over, the one named last changes fastest.
Arguments:
- images: bfloat16 [393216, 1152], P(('dp', 'group')), may hold values from -6 to 6
- texts: bfloat16 [393216, 1152], P(('dp', 'group')), may hold values from -6 to 6
- logit_scale: float32 [1], replicated, may hold values from 40 to 120
- logit_bias: float32 [1], replicated, may hold values from -3 to 3
Outputs:
- row_loss: float32 [393216], P(('dp', 'group'))
- image_grad: bfloat16 [393216, 1152], P(('dp', 'group'))
- text_grad: bfloat16 [393216, 1152], P(('dp', 'group'))
The draws below stay inside these ranges and needn't reach their ends.
All inputs are finite; a program needn't handle non-finite values.
Results may differ from the reference program's by a relative error of at most 0.0075.
Values may be sent and summed in bfloat16 or wider, within the bound.
No kernel may reach another device: no remote copies, remote signals or barrier semaphores. Data moves between devices by JAX's collectives and lax.ppermute only.
A program may use at most 32 MiB of HBM per device.

```python
import math
import jax
import jax.numpy as jnp
from jax import lax

D = 1152
ROWS = 384
PAIRS = 393216


def shard_levels(own_key, shape, split, smallest, high):
    loudness, own = 1.0, jax.random.fold_in(own_key, 6)
    for position, parts in split:
        draws = jnp.exp(jax.random.uniform(jax.random.fold_in(own, position), (parts,), jnp.float32, smallest / len(split), high / len(split)))
        loudness = loudness * jnp.repeat(draws, shape[position] // parts).reshape([-1 if axis == position else 1 for axis in range(len(shape))])
    return loudness


def normal_values(key, extent, scale, most, cuts=(), held_as=jnp.bfloat16):
    array = jax.random.normal(key, extent, jnp.float32) * scale
    if len(cuts) > 0:
        array = shard_levels(key, extent, cuts, -0.22, 0.18) * array
    return jnp.clip(array, min=-most, max=most).astype(held_as)


def setup_inputs(seed: int = 0) -> dict:
    arg_keys = jax.random.split(jax.random.key(seed), 5)
    images = normal_values(arg_keys[0], (PAIRS, D), 1.0, 6.0, ((0, 1024),))
    texts = normal_values(arg_keys[1], (PAIRS, D), 1.0, 6.0, ((0, 1024),))
    logit_scale = jnp.clip(jnp.exp(jax.random.uniform(arg_keys[2], (1,), jnp.float32, math.log(40.0), math.log(120.0))), 40.0, 120.0)
    logit_bias = jnp.clip(jax.random.uniform(arg_keys[3], (1,), jnp.float32, -3.0, 3.0), -3.0, 3.0)
    return dict(images=images, texts=texts, logit_scale=logit_scale, logit_bias=logit_bias)


def normalize(embedded):
    values = embedded.astype(jnp.float32)
    factor = lax.rsqrt(lax.optimization_barrier(jnp.sum(values * values, axis=1, keepdims=True)) + 1e-06)
    return (values * factor, factor)

def unit_backward(unit_grad, unit, factor):
    inner = lax.optimization_barrier(jnp.sum(unit_grad * unit, axis=1, keepdims=True))
    return (factor * (unit_grad - unit * inner)).astype(jnp.bfloat16)

def pair_block(image_low, text_low, labels, logit_scale, logit_bias):
    logits = logit_scale * jnp.dot(image_low, text_low.T, preferred_element_type=jnp.float32) + logit_bias
    signed = labels * logits
    losses = lax.optimization_barrier(jnp.sum(jax.nn.softplus(-signed), axis=1))
    pair_weights = (-logit_scale * labels * jax.nn.sigmoid(-signed)).astype(jnp.bfloat16)
    image_part = jnp.dot(pair_weights, text_low, preferred_element_type=jnp.float32)
    text_part = jnp.dot(pair_weights.T, image_low, preferred_element_type=jnp.float32)
    return (losses, image_part, text_part)

def reference(images, texts, logit_scale, logit_bias):
    features = images.shape[1]
    blocks = images.shape[0] // ROWS
    image_blocks = images.reshape(blocks, ROWS, features)
    text_blocks = texts.reshape(blocks, ROWS, features)
    scale_value = logit_scale[0]
    bias_value = logit_bias[0]
    diagonal = 2.0 * jnp.eye(ROWS, dtype=jnp.float32) - 1.0
    others = -jnp.ones((ROWS, ROWS), jnp.float32)

    def one_block(block):
        image_unit, image_factor = normalize(image_blocks[block])
        image_low = image_unit.astype(jnp.bfloat16)
        losses = jnp.zeros((ROWS,), jnp.float32)
        image_sum = jnp.zeros((ROWS, features), jnp.float32)
        text_parts = []
        for shift_by in range(3):
            source = ((block - shift_by) % blocks).astype(jnp.int32)
            text_low = normalize(text_blocks[source])[0].astype(jnp.bfloat16)
            labels = diagonal if shift_by == 0 else others
            part_loss, image_part, text_part = pair_block(image_low, text_low, labels, scale_value, bias_value)
            losses = losses + part_loss
            image_sum = image_sum + image_part
            text_parts.append(text_part)
        image_out = unit_backward(image_sum, image_unit, image_factor)
        return (losses / (3.0 * ROWS), image_out, text_parts[0], text_parts[1].astype(jnp.bfloat16), text_parts[2].astype(jnp.bfloat16))
    row_loss, image_grad, own_terms, first_terms, second_terms = lax.map(one_block, jnp.arange(blocks, dtype=jnp.int32))
    totals = own_terms + jnp.roll(first_terms, -1, axis=0).astype(jnp.float32)
    totals = totals + jnp.roll(second_terms, -2, axis=0).astype(jnp.float32)

    def text_block(pieces):
        raw, total = pieces
        text_unit, text_factor = normalize(raw)
        return unit_backward(total, text_unit, text_factor)
    text_grad = lax.map(text_block, (text_blocks, totals))
    return (row_loss.reshape(blocks * ROWS), image_grad.reshape(blocks * ROWS, features), text_grad.reshape(blocks * ROWS, features))
```

```python
import jax
import jax.numpy as jnp
from jax import lax
from jax.sharding import PartitionSpec as P

AXES = ("dp", "group")
RUN = 4
CHUNKS = 1


def within(value, hops):
    count = lax.axis_size(AXES)
    pairs = [
        (base + a, base + b) for base in range(0, count, RUN) for a, b in sorted(hops.items())
    ]
    return lax.ppermute(value, AXES, pairs)


def across(value):
    count = lax.axis_size(AXES)
    pairs = [(p, (p + (2 if p % RUN >= 2 else -2)) % count) for p in range(count)]
    return lax.ppermute(value, AXES, pairs)


def normalize(embedded):
    values = embedded.astype(jnp.float32)
    factor = lax.rsqrt(jnp.sum(values * values, axis=1, keepdims=True) + 1e-06)
    return (values * factor, factor)


def low(embedded):
    return normalize(embedded)[0].astype(jnp.bfloat16)


def unit_backward(unit_grad, unit, factor):
    inner = jnp.sum(unit_grad * unit, axis=1, keepdims=True)
    return (factor * (unit_grad - unit * inner)).astype(jnp.bfloat16)


def logits_of(rows, columns, scale_value, bias_value):
    dots = jnp.einsum("id,jd->ij", rows, columns, preferred_element_type=jnp.float32)
    return scale_value * dots + bias_value


def apply(weights, values):
    return jnp.einsum("ij,jd->id", weights, values, preferred_element_type=jnp.float32)


def negative_pairs(rows, columns, scale_value, bias_value):
    logits = logits_of(rows, columns, scale_value, bias_value)
    losses = jnp.sum(jax.nn.softplus(logits), axis=1)
    weights = (scale_value * jax.nn.sigmoid(logits)).astype(jnp.bfloat16)
    return losses, apply(weights, columns)


def shards(images, texts, logit_scale, logit_bias):
    count_rows = images.shape[0]
    scale_value, bias_value = logit_scale[0], logit_bias[0]
    place = lax.axis_index(AXES) % RUN
    first_half = place < 2
    inner = (place == 1) | (place == 2)
    raw_a = jnp.where(first_half, images, texts)
    raw_b = jnp.where(first_half, texts, images)
    step = count_rows // CHUNKS
    far = [across(raw_a[i * step : (i + 1) * step]) for i in range(CHUNKS)]
    near_two = within(raw_b, {0: 2, 2: 0, 1: 3, 3: 1})
    near_one = within(jnp.where(inner, raw_a, raw_b), {1: 0, 2: 3, 0: 1, 3: 2})
    near_mid = within(raw_b, {2: 1, 1: 2})

    unit_a, factor_a = normalize(raw_a)
    unit_b, factor_b = normalize(raw_b)
    low_a, low_b = unit_a.astype(jnp.bfloat16), unit_b.astype(jnp.bfloat16)

    labels = 2.0 * jnp.eye(count_rows, dtype=jnp.float32) - 1.0
    signed = labels * logits_of(low_a, low_b, scale_value, bias_value)
    plus = jax.nn.softplus(-signed)
    own_loss = jnp.where(first_half, jnp.sum(plus, axis=1), jnp.sum(plus, axis=0))
    weights = (-scale_value * labels * jax.nn.sigmoid(-signed)).astype(jnp.bfloat16)
    grad_a = apply(weights, low_b)
    grad_b = jnp.einsum("ij,id->jd", weights, low_a, preferred_element_type=jnp.float32)

    loss_two, part = negative_pairs(low_b, low(near_two), scale_value, bias_value)
    grad_b = grad_b + part
    early = jnp.where(inner, near_mid, near_one)
    loss_one, part = negative_pairs(low_b, low(early), scale_value, bias_value)
    grad_b = grad_b + part
    out_b = unit_backward(grad_b, unit_b, factor_b)
    loss_b = loss_two + loss_one

    loss_a = jnp.zeros_like(loss_b)
    relayed = [within(piece, {1: 0, 2: 3}) for piece in far]
    for piece in far:
        loss, part = negative_pairs(low_a, low(piece), scale_value, bias_value)
        grad_a, loss_a = grad_a + part, loss_a + loss
    for i, piece in enumerate(relayed):
        late = jnp.where(inner, near_one[i * step : (i + 1) * step], piece)
        loss, part = negative_pairs(low_a, low(late), scale_value, bias_value)
        grad_a, loss_a = grad_a + part, loss_a + loss
    out_a = unit_backward(grad_a, unit_a, factor_a)

    row_loss = (own_loss + jnp.where(first_half, loss_a, loss_b)) / (3.0 * count_rows)
    return (row_loss, jnp.where(first_half, out_a, out_b), jnp.where(first_half, out_b, out_a))


def solution(mesh):
    placed = (P(AXES, None), P(AXES, None), P(), P())
    return jax.shard_map(
        shards,
        mesh=mesh,
        in_specs=placed,
        out_specs=(P(AXES), P(AXES, None), P(AXES, None)),
        check_vma=False,
    )
```

```python
import jax
import jax.numpy as jnp
from jax import lax
from jax.sharding import PartitionSpec as P

AXES = ("dp", "group")
RUN = 4
LAYER = 16
PARTS = ((0, 384),)


def tables(count):
    runs = count // RUN
    far, shift, relay = [], [], []
    middle = [(0, count - 1), (count - 1, 0)]
    for run in range(runs):
        middle += [(run * RUN + 1, run * RUN + 2), (run * RUN + 2, run * RUN + 1)]
        step = run % LAYER == LAYER - 1
        slot = (run + 1 - (LAYER if step else 0)) % runs
        final = (run + 1) % runs
        far += [(run * RUN + y, slot * RUN + y - 2) for y in (2, 3)]
        if step:
            shift += [(slot * RUN + y, final * RUN + y) for y in (0, 1)]
        if final != 0:
            relay += [(slot * RUN + 1, final * RUN)]
        step = run % LAYER == 0
        slot = (run - 1 + (LAYER if step else 0)) % runs
        final = (run - 1) % runs
        far += [(run * RUN + y, slot * RUN + y + 2) for y in (0, 1)]
        if step:
            shift += [(slot * RUN + y, final * RUN + y) for y in (2, 3)]
        if run != 0:
            relay += [(slot * RUN + 2, final * RUN + 3)]
    return far, shift, relay, middle


def within(value, hops):
    count = lax.axis_size(AXES)
    pairs = [
        (base + a, base + b) for base in range(0, count, RUN) for a, b in sorted(hops.items())
    ]
    return lax.ppermute(value, AXES, pairs)


def normalize(embedded):
    values = embedded.astype(jnp.float32)
    factor = lax.rsqrt(jnp.sum(values * values, axis=1, keepdims=True) + 1e-06)
    return (values * factor, factor)


def low(embedded):
    return normalize(embedded)[0].astype(jnp.bfloat16)


def unit_backward(unit_grad, unit, factor):
    inner = jnp.sum(unit_grad * unit, axis=1, keepdims=True)
    return (factor * (unit_grad - unit * inner)).astype(jnp.bfloat16)


def logits_of(rows, columns, scale_value, bias_value):
    dots = jnp.einsum("id,jd->ij", rows, columns, preferred_element_type=jnp.float32)
    return scale_value * dots + bias_value


def apply(weights, values):
    return jnp.einsum("ij,jd->id", weights, values, preferred_element_type=jnp.float32)


def negative_pairs(rows, columns, scale_value, bias_value):
    logits = logits_of(rows, columns, scale_value, bias_value)
    losses = jnp.sum(jax.nn.softplus(logits), axis=1)
    weights = (scale_value * jax.nn.sigmoid(logits)).astype(jnp.bfloat16)
    return losses, apply(weights, columns)


def shards(images, texts, logit_scale, logit_bias):
    count_rows = images.shape[0]
    scale_value, bias_value = logit_scale[0], logit_bias[0]
    index = lax.axis_index(AXES)
    count = lax.axis_size(AXES)
    place, run = index % RUN, index // RUN
    first_half = place < 2
    inner = (place == 1) | (place == 2)
    shifted = jnp.where(first_half, run % LAYER == 0, run % LAYER == LAYER - 1)
    end = (index == 0) | (index == count - 1)
    far_pairs, shift_pairs, relay_pairs, middle_pairs = tables(count)
    raw_a = jnp.where(first_half, images, texts)
    raw_b = jnp.where(first_half, texts, images)
    far = [lax.ppermute(raw_a[a:b], AXES, far_pairs) for a, b in PARTS]
    unit_a, factor_a = normalize(raw_a)
    unit_b, factor_b = normalize(raw_b)
    low_a, low_b = unit_a.astype(jnp.bfloat16), unit_b.astype(jnp.bfloat16)
    near_two = within(low_b, {0: 2, 2: 0, 1: 3, 3: 1})
    near_one = within(jnp.where(inner, low_a, low_b), {1: 0, 2: 3, 0: 1, 3: 2})
    middle = lax.ppermute(jnp.where(inner, low_b, low_a), AXES, middle_pairs)

    labels = 2.0 * jnp.eye(count_rows, dtype=jnp.float32) - 1.0
    signed = labels * logits_of(low_a, low_b, scale_value, bias_value)
    plus = jax.nn.softplus(-signed)
    own_loss = jnp.where(first_half, jnp.sum(plus, axis=1), jnp.sum(plus, axis=0))
    weights = (-scale_value * labels * jax.nn.sigmoid(-signed)).astype(jnp.bfloat16)
    grad_a = apply(weights, low_b)
    grad_b = jnp.einsum("ij,id->jd", weights, low_a, preferred_element_type=jnp.float32)

    loss_two, part = negative_pairs(low_b, near_two, scale_value, bias_value)
    grad_b = grad_b + part
    early = jnp.where(inner, middle, near_one)
    loss_one, part = negative_pairs(low_b, early, scale_value, bias_value)
    grad_b = grad_b + part
    out_b = unit_backward(grad_b, unit_b, factor_b)
    loss_b = loss_two + loss_one

    held = jnp.where(inner, near_one, middle)
    loss_a = jnp.zeros_like(loss_b)
    for (a, b), piece in zip(PARTS, far):
        moved = lax.ppermute(piece, AXES, shift_pairs)
        relayed = lax.ppermute(piece, AXES, relay_pairs)
        two = low(jnp.where(shifted, moved, piece))
        loss, part = negative_pairs(low_a, two, scale_value, bias_value)
        grad_a, loss_a = grad_a + part, loss_a + loss
        one = jnp.where(inner | end, held[a:b], low(relayed))
        loss, part = negative_pairs(low_a, one, scale_value, bias_value)
        grad_a, loss_a = grad_a + part, loss_a + loss
    out_a = unit_backward(grad_a, unit_a, factor_a)

    row_loss = (own_loss + jnp.where(first_half, loss_a, loss_b)) / (3.0 * count_rows)
    return (row_loss, jnp.where(first_half, out_a, out_b), jnp.where(first_half, out_b, out_a))


def solution(mesh):
    placed = (P(AXES, None), P(AXES, None), P(), P())
    return jax.shard_map(
        shards,
        mesh=mesh,
        in_specs=placed,
        out_specs=(P(AXES), P(AXES, None), P(AXES, None)),
        check_vma=False,
    )
```

```python
import jax
import jax.numpy as jnp
from jax import lax
from jax.experimental import pallas as pl
from jax.experimental.pallas import tpu as pltpu
from jax.sharding import PartitionSpec as P

AXES = ("dp", "group")
RUN = 4
LAYER = 16
ROW_STEP = 128
LANES = 128


def tables(count):
    runs = count // RUN
    far, shift, relay, wrap = [], [], [], []
    middle = [(0, count - 1), (count - 1, 0)]
    for run in range(runs):
        middle += [(run * RUN + 1, run * RUN + 2), (run * RUN + 2, run * RUN + 1)]
        step = run % LAYER == LAYER - 1
        slot = (run + 1 - (LAYER if step else 0)) % runs
        final = (run + 1) % runs
        far += [(run * RUN + y, slot * RUN + y - 2) for y in (2, 3)]
        if final == 0:
            wrap += [(run * RUN + y, final * RUN + y - 2) for y in (2, 3)]
        else:
            if step:
                shift += [(slot * RUN + y, final * RUN + y) for y in (0, 1)]
            relay += [(slot * RUN + 1, final * RUN)]
        step = run % LAYER == 0
        slot = (run - 1 + (LAYER if step else 0)) % runs
        final = (run - 1) % runs
        far += [(run * RUN + y, slot * RUN + y + 2) for y in (0, 1)]
        if run == 0:
            wrap += [(run * RUN + y, final * RUN + y + 2) for y in (0, 1)]
        else:
            if step:
                shift += [(slot * RUN + y, final * RUN + y) for y in (2, 3)]
            relay += [(slot * RUN + 2, final * RUN + 3)]
    return far, shift, relay, middle, wrap


def within(value, hops):
    count = lax.axis_size(AXES)
    pairs = [
        (base + a, base + b) for base in range(0, count, RUN) for a, b in sorted(hops.items())
    ]
    return lax.ppermute(value, AXES, pairs)


def normalize(embedded):
    values = embedded.astype(jnp.float32)
    factor = lax.rsqrt(jnp.sum(values * values, axis=1, keepdims=True) + 1e-06)
    return (values * factor, factor)


def low(embedded):
    return normalize(embedded)[0].astype(jnp.bfloat16)


def unit_backward(unit_grad, unit, factor):
    inner = jnp.sum(unit_grad * unit, axis=1, keepdims=True)
    return (factor * (unit_grad - unit * inner)).astype(jnp.bfloat16)


def logits_of(rows, columns, scale_value, bias_value):
    dots = jnp.einsum("id,jd->ij", rows, columns, preferred_element_type=jnp.float32)
    return scale_value * dots + bias_value


def apply(weights, values):
    return jnp.einsum("ij,jd->id", weights, values, preferred_element_type=jnp.float32)


def negative_pairs(rows, columns, scale_value, bias_value):
    logits = logits_of(rows, columns, scale_value, bias_value)
    losses = jnp.sum(jax.nn.softplus(logits), axis=1)
    weights = (scale_value * jax.nn.sigmoid(logits)).astype(jnp.bfloat16)
    return losses, apply(weights, columns)


def finish_kernel(
    choices, constants, relayed, held, low_a, raw_a, factor_a, grad_a, out_b, before, loss_out, image_out, text_out, one
):
    rows = low_a.shape[0]
    scale_value, bias_value = constants[0], constants[1]
    use_held, first_half = choices[0] == 1, choices[1] == 1

    @pl.when(use_held)
    def _():
        one[...] = held[...]

    @pl.when(jnp.logical_not(use_held))
    def _():
        for start in range(0, rows, ROW_STEP):
            at = pl.ds(start, ROW_STEP)
            one[at, :] = low(relayed[at, :])

    def last_rows(a_out, b_out, is_image):
        for start in range(0, rows, ROW_STEP):
            at = pl.ds(start, ROW_STEP)
            dots = lax.dot_general(
                low_a[at, :], one[...], (((1,), (1,)), ((), ())), preferred_element_type=jnp.float32
            )
            logits = scale_value * dots + bias_value
            weights = (scale_value * jax.nn.sigmoid(logits)).astype(jnp.bfloat16)
            part = jnp.dot(weights, one[...], preferred_element_type=jnp.float32)
            factor = factor_a[at, 0:1]
            unit = raw_a[at, :].astype(jnp.float32) * factor
            a_out[at, :] = unit_backward(grad_a[at, :] + part, unit, factor)
            b_out[at, :] = out_b[at, :]
            total = before[:, at]
            if is_image:
                plus = jnp.maximum(logits, 0.0) + jnp.log1p(jnp.exp(-jnp.abs(logits)))
                losses = jnp.sum(plus, axis=1, keepdims=True)
                total = total + jnp.broadcast_to(losses, (ROW_STEP, ROW_STEP)).T[0:1, :]
            loss_out[:, at] = total / (3.0 * rows)

    @pl.when(first_half)
    def _():
        last_rows(image_out, text_out, True)

    @pl.when(jnp.logical_not(first_half))
    def _():
        last_rows(text_out, image_out, False)


def finish(choices, constants, relayed, held, low_a, raw_a, factor_a, grad_a, out_b, before):
    rows, features = low_a.shape
    vmem = pl.BlockSpec(memory_space=pltpu.VMEM)
    smem = pl.BlockSpec(memory_space=pltpu.SMEM)
    loss, image_grad, text_grad = pl.pallas_call(
        finish_kernel,
        out_shape=(
            jax.ShapeDtypeStruct((1, rows), jnp.float32),
            jax.ShapeDtypeStruct((rows, features), jnp.bfloat16),
            jax.ShapeDtypeStruct((rows, features), jnp.bfloat16),
        ),
        in_specs=[smem] * 2 + [vmem] * 8,
        out_specs=(vmem,) * 3,
        scratch_shapes=[pltpu.VMEM((rows, features), jnp.bfloat16)],
        compiler_params=pltpu.CompilerParams(vmem_limit_bytes=24 * 1024 * 1024),
        cost_estimate=pl.CostEstimate(
            flops=4 * rows * rows * features, bytes_accessed=8 * rows * features, transcendentals=3 * rows * rows
        ),
    )(choices, constants, relayed, held, low_a, raw_a, factor_a, grad_a, out_b, before.reshape(1, rows))
    return (loss.reshape(rows), image_grad, text_grad)


def shards(images, texts, logit_scale, logit_bias):
    count_rows = images.shape[0]
    scale_value, bias_value = logit_scale[0], logit_bias[0]
    index = lax.axis_index(AXES)
    count = lax.axis_size(AXES)
    place, run = index % RUN, index // RUN
    first_half = place < 2
    inner = (place == 1) | (place == 2)
    shifted = jnp.where(first_half, run % LAYER == 0, run % LAYER == LAYER - 1)
    end = (index == 0) | (index == count - 1)
    wrapped = jnp.where(first_half, run == 0, run == count // RUN - 1)
    far_pairs, shift_pairs, relay_pairs, middle_pairs, wrap_pairs = tables(count)
    raw_a = lax.optimization_barrier(jnp.where(first_half, images, texts))
    raw_b = jnp.where(first_half, texts, images)
    far = lax.ppermute(raw_a, AXES, far_pairs)
    unit_a, factor_a = normalize(raw_a)
    unit_b, factor_b = normalize(raw_b)
    low_a, low_b = unit_a.astype(jnp.bfloat16), unit_b.astype(jnp.bfloat16)
    near_two = within(low_b, {0: 2, 2: 0, 1: 3, 3: 1})
    near_one = within(jnp.where(inner, low_a, low_b), {1: 0, 2: 3, 0: 1, 3: 2})
    wrap = lax.ppermute(low_a, AXES, wrap_pairs)
    middle = lax.ppermute(jnp.where(inner, low_b, low_a), AXES, middle_pairs)

    labels = 2.0 * jnp.eye(count_rows, dtype=jnp.float32) - 1.0
    signed = labels * logits_of(low_a, low_b, scale_value, bias_value)
    plus = jax.nn.softplus(-signed)
    own_loss = jnp.where(first_half, jnp.sum(plus, axis=1), jnp.sum(plus, axis=0))
    weights = (-scale_value * labels * jax.nn.sigmoid(-signed)).astype(jnp.bfloat16)
    grad_a = apply(weights, low_b)
    grad_b = jnp.einsum("ij,id->jd", weights, low_a, preferred_element_type=jnp.float32)

    relayed = lax.ppermute(far, AXES, relay_pairs)

    loss_two, part = negative_pairs(low_b, near_two, scale_value, bias_value)
    grad_b = grad_b + part
    shift_from, loss_two = lax.optimization_barrier((far, loss_two))
    moved = lax.ppermute(shift_from, AXES, shift_pairs)
    early = jnp.where(inner, middle, near_one)
    loss_one, part = negative_pairs(low_b, early, scale_value, bias_value)
    grad_b = grad_b + part
    out_b = unit_backward(grad_b, unit_b, factor_b)
    loss_b = loss_two + loss_one

    held = jnp.where(inner, near_one, middle)
    two = jnp.where(wrapped, wrap, low(jnp.where(shifted, moved, far)))
    loss_a, part = negative_pairs(low_a, two, scale_value, bias_value)
    grad_a = grad_a + part
    before = own_loss + jnp.where(first_half, loss_a, loss_b)
    choices = jnp.stack([inner | end, first_half]).astype(jnp.int32)
    constants = jnp.stack([scale_value, bias_value])
    factor_wide = jnp.broadcast_to(factor_a, (count_rows, LANES))
    return finish(choices, constants, relayed, held, low_a, raw_a, factor_wide, grad_a, out_b, before)


def solution(mesh):
    placed = (P(AXES, None), P(AXES, None), P(), P())
    return jax.shard_map(
        shards,
        mesh=mesh,
        in_specs=placed,
        out_specs=(P(AXES), P(AXES, None), P(AXES, None)),
        check_vma=False,
    )
```

```python
import jax
import jax.numpy as jnp
from jax import lax
from jax.experimental import pallas as pl
from jax.experimental.pallas import tpu as pltpu
from jax.sharding import PartitionSpec as P

AXES = ("dp", "group")
RUN = 4
LAYER = 16
ROW_STEP = 128
LANES = 128


def tables(count):
    runs = count // RUN
    far, shift, relay, wrap = [], [], [], []
    middle = [(0, count - 1), (count - 1, 0)]
    for run in range(runs):
        middle += [(run * RUN + 1, run * RUN + 2), (run * RUN + 2, run * RUN + 1)]
        step = run % LAYER == LAYER - 1
        slot = (run + 1 - (LAYER if step else 0)) % runs
        final = (run + 1) % runs
        far += [(run * RUN + y, slot * RUN + y - 2) for y in (2, 3)]
        if final == 0:
            wrap += [(run * RUN + y, final * RUN + y - 2) for y in (2, 3)]
        else:
            if step:
                shift += [(slot * RUN + y, final * RUN + y) for y in (0, 1)]
            relay += [(slot * RUN + 1, final * RUN)]
        step = run % LAYER == 0
        slot = (run - 1 + (LAYER if step else 0)) % runs
        final = (run - 1) % runs
        far += [(run * RUN + y, slot * RUN + y + 2) for y in (0, 1)]
        if run == 0:
            wrap += [(run * RUN + y, final * RUN + y + 2) for y in (0, 1)]
        else:
            if step:
                shift += [(slot * RUN + y, final * RUN + y) for y in (2, 3)]
            relay += [(slot * RUN + 2, final * RUN + 3)]
    return far, shift, relay, middle, wrap


def within(value, hops):
    count = lax.axis_size(AXES)
    pairs = [
        (base + a, base + b) for base in range(0, count, RUN) for a, b in sorted(hops.items())
    ]
    return lax.ppermute(value, AXES, pairs)


def normalize(embedded):
    values = embedded.astype(jnp.float32)
    factor = lax.rsqrt(jnp.sum(values * values, axis=1, keepdims=True) + 1e-06)
    return (values * factor, factor)


def low(embedded):
    return normalize(embedded)[0].astype(jnp.bfloat16)


def unit_backward(unit_grad, unit, factor):
    inner = jnp.sum(unit_grad * unit, axis=1, keepdims=True)
    return (factor * (unit_grad - unit * inner)).astype(jnp.bfloat16)


def logits_of(rows, columns, scale_value, bias_value):
    dots = jnp.einsum("id,jd->ij", rows, columns, preferred_element_type=jnp.float32)
    return scale_value * dots + bias_value


def apply(weights, values):
    return jnp.einsum("ij,jd->id", weights, values, preferred_element_type=jnp.float32)


def negative_pairs(rows, columns, scale_value, bias_value):
    logits = logits_of(rows, columns, scale_value, bias_value)
    losses = jnp.sum(jax.nn.softplus(logits), axis=1)
    weights = (scale_value * jax.nn.sigmoid(logits)).astype(jnp.bfloat16)
    return losses, apply(weights, columns)


def finish_kernel(
    choices, constants, relayed, held, low_a, raw_a, factor_a, grad_a, out_b, before, loss_out, image_out, text_out, one
):
    rows = low_a.shape[0]
    scale_value, bias_value = constants[0], constants[1]
    use_held, first_half = choices[0] == 1, choices[1] == 1

    @pl.when(use_held)
    def _():
        one[...] = held[...]

    @pl.when(jnp.logical_not(use_held))
    def _():
        for start in range(0, rows, ROW_STEP):
            at = pl.ds(start, ROW_STEP)
            one[at, :] = low(relayed[at, :])

    def last_rows(a_out, b_out, is_image):
        for start in range(0, rows, ROW_STEP):
            at = pl.ds(start, ROW_STEP)
            dots = lax.dot_general(
                low_a[at, :], one[...], (((1,), (1,)), ((), ())), preferred_element_type=jnp.float32
            )
            logits = scale_value * dots + bias_value
            weights = (scale_value * jax.nn.sigmoid(logits)).astype(jnp.bfloat16)
            part = jnp.dot(weights, one[...], preferred_element_type=jnp.float32)
            factor = factor_a[at, 0:1]
            unit = raw_a[at, :].astype(jnp.float32) * factor
            a_out[at, :] = unit_backward(grad_a[at, :] + part, unit, factor)
            b_out[at, :] = out_b[at, :]
            total = before[:, at]
            if is_image:
                plus = jnp.maximum(logits, 0.0) + jnp.log1p(jnp.exp(-jnp.abs(logits)))
                losses = jnp.sum(plus, axis=1, keepdims=True)
                total = total + jnp.broadcast_to(losses, (ROW_STEP, ROW_STEP)).T[0:1, :]
            loss_out[:, at] = total / (3.0 * rows)

    @pl.when(first_half)
    def _():
        last_rows(image_out, text_out, True)

    @pl.when(jnp.logical_not(first_half))
    def _():
        last_rows(text_out, image_out, False)


def finish(choices, constants, relayed, held, low_a, raw_a, factor_a, grad_a, out_b, before):
    rows, features = low_a.shape
    vmem = pl.BlockSpec(memory_space=pltpu.VMEM)
    smem = pl.BlockSpec(memory_space=pltpu.SMEM)
    loss, image_grad, text_grad = pl.pallas_call(
        finish_kernel,
        out_shape=(
            jax.ShapeDtypeStruct((1, rows), jnp.float32),
            jax.ShapeDtypeStruct((rows, features), jnp.bfloat16),
            jax.ShapeDtypeStruct((rows, features), jnp.bfloat16),
        ),
        in_specs=[smem] * 2 + [vmem] * 8,
        out_specs=(vmem,) * 3,
        scratch_shapes=[pltpu.VMEM((rows, features), jnp.bfloat16)],
        compiler_params=pltpu.CompilerParams(vmem_limit_bytes=24 * 1024 * 1024),
        cost_estimate=pl.CostEstimate(
            flops=4 * rows * rows * features, bytes_accessed=8 * rows * features, transcendentals=3 * rows * rows
        ),
    )(choices, constants, relayed, held, low_a, raw_a, factor_a, grad_a, out_b, before.reshape(1, rows))
    return (loss.reshape(rows), image_grad, text_grad)


def shards(images, texts, logit_scale, logit_bias):
    count_rows = images.shape[0]
    scale_value, bias_value = logit_scale[0], logit_bias[0]
    index = lax.axis_index(AXES)
    count = lax.axis_size(AXES)
    place, run = index % RUN, index // RUN
    first_half = place < 2
    inner = (place == 1) | (place == 2)
    shifted = jnp.where(first_half, run % LAYER == 0, run % LAYER == LAYER - 1)
    end = (index == 0) | (index == count - 1)
    wrapped = jnp.where(first_half, run == 0, run == count // RUN - 1)
    far_pairs, shift_pairs, relay_pairs, middle_pairs, wrap_pairs = tables(count)
    raw_a = lax.optimization_barrier(jnp.where(first_half, images, texts))
    raw_b = jnp.where(first_half, texts, images)
    far = lax.ppermute(raw_a, AXES, far_pairs)
    unit_a, factor_a = normalize(raw_a)
    unit_b, factor_b = normalize(raw_b)
    low_a, low_b = unit_a.astype(jnp.bfloat16), unit_b.astype(jnp.bfloat16)
    near_two = within(low_b, {0: 2, 2: 0, 1: 3, 3: 1})
    near_one = within(jnp.where(inner, low_a, low_b), {1: 0, 2: 3, 0: 1, 3: 2})
    wrap = lax.ppermute(low_a, AXES, wrap_pairs)
    middle = lax.ppermute(jnp.where(inner, low_b, low_a), AXES, middle_pairs)

    labels = 2.0 * jnp.eye(count_rows, dtype=jnp.float32) - 1.0
    signed = labels * logits_of(low_a, low_b, scale_value, bias_value)
    plus = jax.nn.softplus(-signed)
    own_loss = jnp.where(first_half, jnp.sum(plus, axis=1), jnp.sum(plus, axis=0))
    weights = (-scale_value * labels * jax.nn.sigmoid(-signed)).astype(jnp.bfloat16)
    grad_a = apply(weights, low_b)
    grad_b = jnp.einsum("ij,id->jd", weights, low_a, preferred_element_type=jnp.float32)


    loss_two, part = negative_pairs(low_b, near_two, scale_value, bias_value)
    grad_b = grad_b + part
    early = jnp.where(inner, middle, near_one)
    loss_one, part = negative_pairs(low_b, early, scale_value, bias_value)
    grad_b = grad_b + part
    out_b = unit_backward(grad_b, unit_b, factor_b)
    loss_b = loss_two + loss_one
    far, loss_b = lax.optimization_barrier((far, loss_b))
    relayed = lax.ppermute(far, AXES, relay_pairs)
    shift_from, low_far = lax.optimization_barrier((far, low(far)))
    moved = lax.ppermute(shift_from, AXES, shift_pairs)

    held = jnp.where(inner, near_one, middle)
    two = jnp.where(wrapped, wrap, jnp.where(shifted, low(moved), low_far))
    loss_a, part = negative_pairs(low_a, two, scale_value, bias_value)
    grad_a = grad_a + part
    before = own_loss + jnp.where(first_half, loss_a, loss_b)
    choices = jnp.stack([inner | end, first_half]).astype(jnp.int32)
    constants = jnp.stack([scale_value, bias_value])
    factor_wide = jnp.broadcast_to(factor_a, (count_rows, LANES))
    return finish(choices, constants, relayed, held, low_a, raw_a, factor_wide, grad_a, out_b, before)


def solution(mesh):
    placed = (P(AXES, None), P(AXES, None), P(), P())
    return jax.shard_map(
        shards,
        mesh=mesh,
        in_specs=placed,
        out_specs=(P(AXES), P(AXES, None), P(AXES, None)),
        check_vma=False,
    )
```

```python
import jax
import jax.numpy as jnp
from jax import lax
from jax.experimental import pallas as pl
from jax.experimental.pallas import tpu as pltpu
from jax.sharding import PartitionSpec as P

AXES = ("dp", "group")
RUN = 4
LAYER = 16
ROW_STEP = 384
LANES = 128


def tables(count):
    runs = count // RUN
    far, shift, relay, wrap = [], [], [], []
    middle = [(0, count - 1), (count - 1, 0)]
    for run in range(runs):
        middle += [(run * RUN + 1, run * RUN + 2), (run * RUN + 2, run * RUN + 1)]
        step = run % LAYER == LAYER - 1
        slot = (run + 1 - (LAYER if step else 0)) % runs
        final = (run + 1) % runs
        far += [(run * RUN + y, slot * RUN + y - 2) for y in (2, 3)]
        if final == 0:
            wrap += [(run * RUN + y, final * RUN + y - 2) for y in (2, 3)]
        else:
            if step:
                shift += [(slot * RUN + y, final * RUN + y) for y in (0, 1)]
            relay += [(slot * RUN + 1, final * RUN)]
        step = run % LAYER == 0
        slot = (run - 1 + (LAYER if step else 0)) % runs
        final = (run - 1) % runs
        far += [(run * RUN + y, slot * RUN + y + 2) for y in (0, 1)]
        if run == 0:
            wrap += [(run * RUN + y, final * RUN + y + 2) for y in (0, 1)]
        else:
            if step:
                shift += [(slot * RUN + y, final * RUN + y) for y in (2, 3)]
            relay += [(slot * RUN + 2, final * RUN + 3)]
    return far, shift, relay, middle, wrap


def within(value, hops):
    count = lax.axis_size(AXES)
    pairs = [
        (base + a, base + b) for base in range(0, count, RUN) for a, b in sorted(hops.items())
    ]
    return lax.ppermute(value, AXES, pairs)


def normalize(embedded):
    values = embedded.astype(jnp.float32)
    factor = lax.rsqrt(jnp.sum(values * values, axis=1, keepdims=True) + 1e-06)
    return (values * factor, factor)


def low(embedded):
    return normalize(embedded)[0].astype(jnp.bfloat16)


def unit_backward(unit_grad, unit, factor):
    inner = jnp.sum(unit_grad * unit, axis=1, keepdims=True)
    return (factor * (unit_grad - unit * inner)).astype(jnp.bfloat16)


def logits_of(rows, columns, scale_value, bias_value):
    dots = jnp.einsum("id,jd->ij", rows, columns, preferred_element_type=jnp.float32)
    return scale_value * dots + bias_value


def apply(weights, values):
    return jnp.einsum("ij,jd->id", weights, values, preferred_element_type=jnp.float32)


def negative_pairs(rows, columns, scale_value, bias_value):
    logits = logits_of(rows, columns, scale_value, bias_value)
    losses = jnp.sum(jax.nn.softplus(logits), axis=1)
    weights = (scale_value * jax.nn.sigmoid(logits)).astype(jnp.bfloat16)
    return losses, apply(weights, columns)


def finish_kernel(
    choices, constants, relayed, held, low_a, raw_a, factor_a, grad_a, out_b, before, loss_out, image_out, text_out, one
):
    rows = low_a.shape[0]
    scale_value, bias_value = constants[0], constants[1]
    use_held, first_half = choices[0] == 1, choices[1] == 1

    @pl.when(use_held)
    def _():
        one[...] = held[...]

    @pl.when(jnp.logical_not(use_held))
    def _():
        for start in range(0, rows, ROW_STEP):
            at = pl.ds(start, ROW_STEP)
            one[at, :] = low(relayed[at, :])

    def last_rows(a_out, b_out, is_image):
        for start in range(0, rows, ROW_STEP):
            at = pl.ds(start, ROW_STEP)
            dots = lax.dot_general(
                low_a[at, :], one[...], (((1,), (1,)), ((), ())), preferred_element_type=jnp.float32
            )
            logits = scale_value * dots + bias_value
            decay = jnp.exp(-jnp.abs(logits))
            chance = jnp.where(logits >= 0.0, 1.0, decay) / (1.0 + decay)
            weights = (scale_value * chance).astype(jnp.bfloat16)
            part = jnp.dot(weights, one[...], preferred_element_type=jnp.float32)
            factor = factor_a[at, 0:1]
            unit = raw_a[at, :].astype(jnp.float32) * factor
            a_out[at, :] = unit_backward(grad_a[at, :] + part, unit, factor)
            b_out[at, :] = out_b[at, :]
            total = before[:, at]
            if is_image:
                plus = jnp.maximum(logits, 0.0) + jnp.log1p(decay)
                losses = jnp.sum(plus, axis=1, keepdims=True)
                total = total + jnp.broadcast_to(losses, (ROW_STEP, ROW_STEP)).T[0:1, :]
            loss_out[:, at] = total / (3.0 * rows)

    @pl.when(first_half)
    def _():
        last_rows(image_out, text_out, True)

    @pl.when(jnp.logical_not(first_half))
    def _():
        last_rows(text_out, image_out, False)


def finish(choices, constants, relayed, held, low_a, raw_a, factor_a, grad_a, out_b, before):
    rows, features = low_a.shape
    vmem = pl.BlockSpec(memory_space=pltpu.VMEM)
    smem = pl.BlockSpec(memory_space=pltpu.SMEM)
    loss, image_grad, text_grad = pl.pallas_call(
        finish_kernel,
        out_shape=(
            jax.ShapeDtypeStruct((1, rows), jnp.float32),
            jax.ShapeDtypeStruct((rows, features), jnp.bfloat16),
            jax.ShapeDtypeStruct((rows, features), jnp.bfloat16),
        ),
        in_specs=[smem] * 2 + [vmem] * 8,
        out_specs=(vmem,) * 3,
        scratch_shapes=[pltpu.VMEM((rows, features), jnp.bfloat16)],
        compiler_params=pltpu.CompilerParams(vmem_limit_bytes=24 * 1024 * 1024),
        cost_estimate=pl.CostEstimate(
            flops=4 * rows * rows * features, bytes_accessed=8 * rows * features, transcendentals=3 * rows * rows
        ),
    )(choices, constants, relayed, held, low_a, raw_a, factor_a, grad_a, out_b, before.reshape(1, rows))
    return (loss.reshape(rows), image_grad, text_grad)


def shards(images, texts, logit_scale, logit_bias):
    count_rows = images.shape[0]
    scale_value, bias_value = logit_scale[0], logit_bias[0]
    index = lax.axis_index(AXES)
    count = lax.axis_size(AXES)
    place, run = index % RUN, index // RUN
    first_half = place < 2
    inner = (place == 1) | (place == 2)
    shifted = jnp.where(first_half, run % LAYER == 0, run % LAYER == LAYER - 1)
    end = (index == 0) | (index == count - 1)
    wrapped = jnp.where(first_half, run == 0, run == count // RUN - 1)
    far_pairs, shift_pairs, relay_pairs, middle_pairs, wrap_pairs = tables(count)
    raw_a = lax.optimization_barrier(jnp.where(first_half, images, texts))
    raw_b = jnp.where(first_half, texts, images)
    far = lax.ppermute(raw_a, AXES, far_pairs)
    unit_a, factor_a = normalize(raw_a)
    unit_b, factor_b = normalize(raw_b)
    low_a, low_b = unit_a.astype(jnp.bfloat16), unit_b.astype(jnp.bfloat16)
    near_two = within(low_b, {0: 2, 2: 0, 1: 3, 3: 1})
    near_one = within(jnp.where(inner, low_a, low_b), {1: 0, 2: 3, 0: 1, 3: 2})
    wrap = lax.ppermute(low_a, AXES, wrap_pairs)
    middle = lax.ppermute(jnp.where(inner, low_b, low_a), AXES, middle_pairs)

    labels = 2.0 * jnp.eye(count_rows, dtype=jnp.float32) - 1.0
    signed = labels * logits_of(low_a, low_b, scale_value, bias_value)
    plus = jax.nn.softplus(-signed)
    own_loss = jnp.where(first_half, jnp.sum(plus, axis=1), jnp.sum(plus, axis=0))
    weights = (-scale_value * labels * jax.nn.sigmoid(-signed)).astype(jnp.bfloat16)
    grad_a = apply(weights, low_b)
    grad_b = jnp.einsum("ij,id->jd", weights, low_a, preferred_element_type=jnp.float32)

    relayed = lax.ppermute(far, AXES, relay_pairs)

    loss_two, part = negative_pairs(low_b, near_two, scale_value, bias_value)
    grad_b = grad_b + part
    shift_from, loss_two = lax.optimization_barrier((far, loss_two))
    moved = lax.ppermute(shift_from, AXES, shift_pairs)
    early = jnp.where(inner, middle, near_one)
    loss_one, part = negative_pairs(low_b, early, scale_value, bias_value)
    grad_b = grad_b + part
    out_b = unit_backward(grad_b, unit_b, factor_b)
    loss_b = loss_two + loss_one

    held = jnp.where(inner, near_one, middle)
    two = jnp.where(wrapped, wrap, low(jnp.where(shifted, moved, far)))
    loss_a, part = negative_pairs(low_a, two, scale_value, bias_value)
    grad_a = grad_a + part
    before = own_loss + jnp.where(first_half, loss_a, loss_b)
    choices = jnp.stack([inner | end, first_half]).astype(jnp.int32)
    constants = jnp.stack([scale_value, bias_value])
    factor_wide = jnp.broadcast_to(factor_a, (count_rows, LANES))
    return finish(choices, constants, relayed, held, low_a, raw_a, factor_wide, grad_a, out_b, before)


def solution(mesh):
    placed = (P(AXES, None), P(AXES, None), P(), P())
    return jax.shard_map(
        shards,
        mesh=mesh,
        in_specs=placed,
        out_specs=(P(AXES), P(AXES, None), P(AXES, None)),
        check_vma=False,
    )
```

```python
import jax
import jax.numpy as jnp
from jax import lax
from jax.experimental import pallas as pl
from jax.experimental.pallas import tpu as pltpu
from jax.sharding import PartitionSpec as P

AXES = ("dp", "group")
RUN = 4
LAYER = 16
ROW_STEP = 128
SPLIT = 256
LANES = 128


def tables(count):
    runs = count // RUN
    far, shift, relay, wrap = [], [], [], []
    middle = [(0, count - 1), (count - 1, 0)]
    for run in range(runs):
        middle += [(run * RUN + 1, run * RUN + 2), (run * RUN + 2, run * RUN + 1)]
        step = run % LAYER == LAYER - 1
        slot = (run + 1 - (LAYER if step else 0)) % runs
        final = (run + 1) % runs
        far += [(run * RUN + y, slot * RUN + y - 2) for y in (2, 3)]
        if final == 0:
            wrap += [(run * RUN + y, final * RUN + y - 2) for y in (2, 3)]
        else:
            if step:
                shift += [(slot * RUN + y, final * RUN + y) for y in (0, 1)]
            relay += [(slot * RUN + 1, final * RUN)]
        step = run % LAYER == 0
        slot = (run - 1 + (LAYER if step else 0)) % runs
        final = (run - 1) % runs
        far += [(run * RUN + y, slot * RUN + y + 2) for y in (0, 1)]
        if run == 0:
            wrap += [(run * RUN + y, final * RUN + y + 2) for y in (0, 1)]
        else:
            if step:
                shift += [(slot * RUN + y, final * RUN + y) for y in (2, 3)]
            relay += [(slot * RUN + 2, final * RUN + 3)]
    return far, shift, relay, middle, wrap


def within(value, hops):
    count = lax.axis_size(AXES)
    pairs = [
        (base + a, base + b) for base in range(0, count, RUN) for a, b in sorted(hops.items())
    ]
    return lax.ppermute(value, AXES, pairs)


def normalize(embedded):
    values = embedded.astype(jnp.float32)
    factor = lax.rsqrt(jnp.sum(values * values, axis=1, keepdims=True) + 1e-06)
    return (values * factor, factor)


def low(embedded):
    return normalize(embedded)[0].astype(jnp.bfloat16)


def unit_backward(unit_grad, unit, factor):
    inner = jnp.sum(unit_grad * unit, axis=1, keepdims=True)
    return (factor * (unit_grad - unit * inner)).astype(jnp.bfloat16)


def logits_of(rows, columns, scale_value, bias_value):
    dots = jnp.einsum("id,jd->ij", rows, columns, preferred_element_type=jnp.float32)
    return scale_value * dots + bias_value


def apply(weights, values):
    return jnp.einsum("ij,jd->id", weights, values, preferred_element_type=jnp.float32)


def negative_pairs(rows, columns, scale_value, bias_value):
    logits = logits_of(rows, columns, scale_value, bias_value)
    losses = jnp.sum(jax.nn.softplus(logits), axis=1)
    weights = (scale_value * jax.nn.sigmoid(logits)).astype(jnp.bfloat16)
    return losses, apply(weights, columns)


def finish_kernel(
    choices, constants, relayed, held, low_a, raw_a, factor_a, grad_a, out_b, before, loss_out, image_out, text_out, one
):
    rows = low_a.shape[0]
    scale_value, bias_value = constants[0], constants[1]
    use_held, first_half = choices[0] == 1, choices[1] == 1

    @pl.when(use_held)
    def _():
        one[...] = held[...]

    @pl.when(jnp.logical_not(use_held))
    def _():
        for start in range(0, one.shape[0], ROW_STEP):
            at = pl.ds(start, ROW_STEP)
            one[at, :] = low(relayed[at, :])

    def last_rows(a_out, b_out, is_image):
        for start in range(0, rows, ROW_STEP):
            at = pl.ds(start, ROW_STEP)
            dots = lax.dot_general(
                low_a[at, :], one[...], (((1,), (1,)), ((), ())), preferred_element_type=jnp.float32
            )
            logits = scale_value * dots + bias_value
            weights = (scale_value * jax.nn.sigmoid(logits)).astype(jnp.bfloat16)
            part = jnp.dot(weights, one[...], preferred_element_type=jnp.float32)
            factor = factor_a[at, 0:1]
            unit = raw_a[at, :].astype(jnp.float32) * factor
            a_out[at, :] = unit_backward(grad_a[at, :] + part, unit, factor)
            b_out[at, :] = out_b[at, :]
            total = before[:, at]
            if is_image:
                plus = jnp.maximum(logits, 0.0) + jnp.log1p(jnp.exp(-jnp.abs(logits)))
                losses = jnp.sum(plus, axis=1, keepdims=True)
                total = total + jnp.broadcast_to(losses, (ROW_STEP, ROW_STEP)).T[0:1, :]
            loss_out[:, at] = total / (3.0 * rows)

    @pl.when(first_half)
    def _():
        last_rows(image_out, text_out, True)

    @pl.when(jnp.logical_not(first_half))
    def _():
        last_rows(text_out, image_out, False)


def finish(choices, constants, relayed, held, low_a, raw_a, factor_a, grad_a, out_b, before):
    rows, features = low_a.shape
    vmem = pl.BlockSpec(memory_space=pltpu.VMEM)
    smem = pl.BlockSpec(memory_space=pltpu.SMEM)
    loss, image_grad, text_grad = pl.pallas_call(
        finish_kernel,
        out_shape=(
            jax.ShapeDtypeStruct((1, rows), jnp.float32),
            jax.ShapeDtypeStruct((rows, features), jnp.bfloat16),
            jax.ShapeDtypeStruct((rows, features), jnp.bfloat16),
        ),
        in_specs=[smem] * 2 + [vmem] * 8,
        out_specs=(vmem,) * 3,
        scratch_shapes=[pltpu.VMEM(relayed.shape, jnp.bfloat16)],
        compiler_params=pltpu.CompilerParams(vmem_limit_bytes=24 * 1024 * 1024),
        cost_estimate=pl.CostEstimate(
            flops=4 * rows * held.shape[0] * features,
            bytes_accessed=8 * rows * features,
            transcendentals=3 * rows * held.shape[0],
        ),
    )(choices, constants, relayed, held, low_a, raw_a, factor_a, grad_a, out_b, before.reshape(1, rows))
    return (loss.reshape(rows), image_grad, text_grad)


def shards(images, texts, logit_scale, logit_bias):
    count_rows = images.shape[0]
    scale_value, bias_value = logit_scale[0], logit_bias[0]
    index = lax.axis_index(AXES)
    count = lax.axis_size(AXES)
    place, run = index % RUN, index // RUN
    first_half = place < 2
    inner = (place == 1) | (place == 2)
    shifted = jnp.where(first_half, run % LAYER == 0, run % LAYER == LAYER - 1)
    end = (index == 0) | (index == count - 1)
    wrapped = jnp.where(first_half, run == 0, run == count // RUN - 1)
    far_pairs, shift_pairs, relay_pairs, middle_pairs, wrap_pairs = tables(count)
    raw_a = lax.optimization_barrier(jnp.where(first_half, images, texts))
    raw_b = jnp.where(first_half, texts, images)
    far = lax.ppermute(raw_a, AXES, far_pairs)
    unit_a, factor_a = normalize(raw_a)
    unit_b, factor_b = normalize(raw_b)
    low_a, low_b = unit_a.astype(jnp.bfloat16), unit_b.astype(jnp.bfloat16)
    near_two = within(low_b, {0: 2, 2: 0, 1: 3, 3: 1})
    near_one = within(jnp.where(inner, low_a, low_b), {1: 0, 2: 3, 0: 1, 3: 2})
    wrap = lax.ppermute(low_a, AXES, wrap_pairs)
    middle = lax.ppermute(jnp.where(inner, low_b, low_a), AXES, middle_pairs)

    labels = 2.0 * jnp.eye(count_rows, dtype=jnp.float32) - 1.0
    signed = labels * logits_of(low_a, low_b, scale_value, bias_value)
    plus = jax.nn.softplus(-signed)
    own_loss = jnp.where(first_half, jnp.sum(plus, axis=1), jnp.sum(plus, axis=0))
    weights = (-scale_value * labels * jax.nn.sigmoid(-signed)).astype(jnp.bfloat16)
    grad_a = apply(weights, low_b)
    grad_b = jnp.einsum("ij,id->jd", weights, low_a, preferred_element_type=jnp.float32)

    relayed = [lax.ppermute(rows, AXES, relay_pairs) for rows in (far[:SPLIT], far[SPLIT:])]
    shift_from, low_far = lax.optimization_barrier((far, low(far)))
    moved = lax.ppermute(shift_from, AXES, shift_pairs)

    loss_two, part = negative_pairs(low_b, near_two, scale_value, bias_value)
    grad_b = grad_b + part
    early = jnp.where(inner, middle, near_one)
    loss_one, part = negative_pairs(low_b, early, scale_value, bias_value)
    grad_b = grad_b + part
    out_b = unit_backward(grad_b, unit_b, factor_b)
    loss_b = loss_two + loss_one

    held = jnp.where(inner, near_one, middle)
    two = jnp.where(wrapped, wrap, jnp.where(shifted, low(moved), low_far))
    loss_a, part = negative_pairs(low_a, two, scale_value, bias_value)
    grad_a = grad_a + part
    use_held = inner | end
    one = jnp.where(use_held, held[:SPLIT], low(relayed[0]))
    loss, part = negative_pairs(low_a, one, scale_value, bias_value)
    grad_a, loss_a = grad_a + part, loss_a + loss
    before = own_loss + jnp.where(first_half, loss_a, loss_b)
    choices = jnp.stack([use_held, first_half]).astype(jnp.int32)
    constants = jnp.stack([scale_value, bias_value])
    factor_wide = jnp.broadcast_to(factor_a, (count_rows, LANES))
    last, grad_a, before, factor_wide = lax.optimization_barrier((relayed[1], grad_a, before, factor_wide))
    return finish(choices, constants, last, held[SPLIT:], low_a, raw_a, factor_wide, grad_a, out_b, before)


def solution(mesh):
    placed = (P(AXES, None), P(AXES, None), P(), P())
    return jax.shard_map(
        shards,
        mesh=mesh,
        in_specs=placed,
        out_specs=(P(AXES), P(AXES, None), P(AXES, None)),
        check_vma=False,
    )
```
